32 devices in a mesh: dist: 8 (over y, x, core), mem: 4 (over z).
Axes of the slice: x: 2, y: 2, z: 4, core: 2. Of those that a mesh axis runs over, the one named last changes fastest.
Arguments:
- anomalies: bfloat16 [64, 2048, 512], P('dist', None, 'mem'), may hold values from -6 to 6
- innovations: bfloat16 [64, 256, 512], P('dist', None, 'mem'), may hold values from -6 to 6
- obs_var: bfloat16 [64, 256], P('dist'), may hold values from 0.25 to 2
- node_pos: bfloat16 [2, 64, 2048], P(None, 'dist'), may hold values from 0 to 1
- obs_node: int32 [64, 256], P('dist'), may hold values from 0 to 2047
- obs_count: int32 [64], P('dist'), may hold values from 64 to 256, as said below
- in_radius: int32 [64, 7], P('dist'), may hold values from 0 to 1, as said below
Outputs:
- increment: float32 [64, 2048, 512], P('dist', 'mem')
The draws below stay inside these ranges and needn't reach their ends.
Inputs may be any that keep to these rules, and one draw needn't show every extreme that they name: `obs_count`: every district has at least 64 observations in use, and some district has all 256. `in_radius`: slot 3 (the district itself) is always 1; the ones of a district form a band of slots around it; slots naming a district outside 0 to 63 are 0; some district is paired with all districts up to 3 away.
All inputs are finite; a program needn't handle non-finite values.
Results may differ from the reference program's by a relative error of at most 0.0029.
Values may be sent and summed in bfloat16 or wider, within the bound.
No kernel may reach another device: no remote copies, remote signals or barrier semaphores. Data moves between devices by JAX's collectives and lax.ppermute only.
A program may use at most 192 MiB of HBM per device.

```python
import math
import jax
import jax.numpy as jnp
from jax import lax

NODES = 2048
OBS_CAP = 256
RADIUS = 3
MEMBERS = 512
DISTRICTS = 64


def draw_obs_count(key, part):
    key_counts, key_top = jax.random.split(jax.random.fold_in(key, 11))
    counts = jax.random.randint(key_counts, (DISTRICTS,), OBS_CAP // 4, OBS_CAP + 1, dtype=jnp.int32)
    top_district = jax.random.randint(key_top, (), 0, DISTRICTS, dtype=jnp.int32)
    return counts.at[top_district].set(OBS_CAP)


def draw_in_radius(key, part):
    key_first, key_second, key_top = jax.random.split(jax.random.fold_in(key, 23), 3)
    first_reach = jax.random.randint(key_first, (DISTRICTS,), 0, RADIUS + 1, dtype=jnp.int32)
    second_reach = jax.random.randint(key_second, (DISTRICTS,), 0, RADIUS + 1, dtype=jnp.int32)
    reach = jnp.minimum(first_reach, second_reach)
    top_district = jax.random.randint(key_top, (), 0, DISTRICTS, dtype=jnp.int32)
    reach = reach.at[top_district].set(RADIUS)
    offsets = jnp.arange(2 * RADIUS + 1, dtype=jnp.int32) - RADIUS
    partner = jnp.arange(DISTRICTS, dtype=jnp.int32)[:, None] + offsets[None, :]
    inside = (jnp.abs(offsets)[None, :] <= reach[:, None]) & (partner >= 0) & (partner < DISTRICTS)
    return inside.astype(jnp.int32)


def with_ends(array, stream_key, smallest, largest):
    dims = array.shape
    spot = [jax.random.randint(jax.random.fold_in(stream_key, axis), (), 0, dims[axis]) for axis in range(len(dims))]
    array = array.at[tuple(spot)].set(smallest)
    longest = dims.index(max(dims))
    spot[longest] = (spot[longest] + 1) % dims[longest]
    return array.at[tuple(spot)].set(largest)


def levels(own_key, extent, cuts, smallest, top_value):
    level, own = 1.0, jax.random.fold_in(own_key, 6)
    for dim, shards_of in cuts:
        heights = jnp.exp(jax.random.uniform(jax.random.fold_in(own, dim), (shards_of,), jnp.float32, smallest / len(cuts), top_value / len(cuts)))
        level = level * jnp.repeat(heights, extent[dim] // shards_of).reshape([-1 if axis == dim else 1 for axis in range(len(extent))])
    return level


def scatter_about(stream_key, extent, scale, most, cuts=(), held_as=jnp.bfloat16):
    level = levels(stream_key, extent, cuts, -0.22, 0.18) if cuts else 1.0
    result = jax.random.normal(stream_key, extent, jnp.float32) * scale * level
    return jnp.minimum(jnp.maximum(result, -most), most).astype(held_as)


def setup_inputs(seed: int = 0) -> dict:
    streams_of = jax.random.split(jax.random.key(seed), 8)
    anomalies = scatter_about(streams_of[0], (DISTRICTS, NODES, MEMBERS), 1.0, 6.0, ((0, 8), (2, 4)))
    innovations = scatter_about(streams_of[1], (DISTRICTS, OBS_CAP, MEMBERS), 1.0, 6.0, ((0, 8), (2, 4)))
    obs_var = jnp.clip(jnp.exp(math.log(2.0) - 2.0794415 * jax.random.uniform(streams_of[2], (DISTRICTS, OBS_CAP), jnp.float32) ** levels(streams_of[2], (DISTRICTS, OBS_CAP), ((0, 8),), -0.2, 0.2)), 0.25, 2.0).astype(jnp.bfloat16)
    node_pos = jnp.clip(1.0 * jax.random.uniform(streams_of[3], (2, DISTRICTS, NODES), jnp.float32) ** levels(streams_of[3], (2, DISTRICTS, NODES), ((1, 8),), -0.2, 0.2), 0.0, 1.0).astype(jnp.bfloat16)
    obs_node = with_ends(jax.random.randint(streams_of[4], (DISTRICTS, OBS_CAP), 0, NODES), jax.random.fold_in(streams_of[4], 1), 0, NODES - 1).astype(jnp.int32)
    obs_count = draw_obs_count(jax.random.fold_in(streams_of[7], 71), 0)
    in_radius = draw_in_radius(jax.random.fold_in(streams_of[7], 71), 0)
    return dict(anomalies=anomalies, innovations=innovations, obs_var=obs_var, node_pos=node_pos, obs_node=obs_node, obs_count=obs_count, in_radius=in_radius)


def gc_taper(ratio):
    square = ratio * ratio
    cubed = square * ratio
    fourth = cubed * ratio
    fifth_power = fourth * ratio
    inner_part = -0.25 * fifth_power + 0.5 * fourth + 0.625 * cubed - 5.0 / 3.0 * square + 1.0
    clipped = jnp.maximum(ratio, 1.0)
    outer_part = fifth_power / 12.0 - 0.5 * fourth + 0.625 * cubed + 5.0 / 3.0 * square - 5.0 * ratio + 4.0 - 2.0 / (3.0 * clipped)
    return jnp.where(ratio < 1.0, inner_part, jnp.where(ratio < 2.0, outer_part, 0.0))

def pair_gain(x_rows, obs_rows, node_xy, obs_xy, spread_row, offset, members):
    node_xy = node_xy.astype(jnp.float32)
    obs_xy = obs_xy.astype(jnp.float32)
    delta_x = offset + obs_xy[0][None, :] - node_xy[0][:, None]
    delta_y = obs_xy[1][None, :] - node_xy[1][:, None]
    distance = jnp.sqrt(delta_x * delta_x + delta_y * delta_y)
    weight = gc_taper(distance / ((RADIUS + 2) / 2.0))
    covariance = lax.dot_general(x_rows, obs_rows, (((1,), (1,)), ((), ())), preferred_element_type=jnp.float32) / (members - 1)
    return (weight * covariance / spread_row[None, :]).astype(jnp.bfloat16)

def pick_rows(table, index):
    return table[index]

def pick_columns(table, index):
    return table[:, index]

def reference(anomalies, innovations, obs_var, node_pos, obs_node, obs_count, in_radius):
    members = anomalies.shape[2]
    live_slot = jnp.arange(OBS_CAP, dtype=jnp.int32)[None, :] < obs_count[:, None]
    picked = jax.vmap(pick_rows)(anomalies, obs_node)
    observed = jnp.where(live_slot[:, :, None], picked, jnp.zeros((), jnp.bfloat16))
    obs_xy = jax.vmap(pick_columns, in_axes=(1, 0), out_axes=1)(node_pos, obs_node)
    spread = lax.optimization_barrier(jnp.sum(jnp.square(observed.astype(jnp.float32)), axis=2)) / (members - 1) + obs_var.astype(jnp.float32)

    def one_district(district):
        x_rows = lax.dynamic_index_in_dim(anomalies, district, 0, keepdims=False)
        node_xy = lax.dynamic_index_in_dim(node_pos, district, 1, keepdims=False)
        total = jnp.zeros((NODES, members), jnp.float32)
        for slot in range(2 * RADIUS + 1):
            other = jnp.clip(district + slot - RADIUS, 0, DISTRICTS - 1).astype(jnp.int32)

            def accumulate(current, other=other, slot=slot):
                obs_rows = lax.dynamic_index_in_dim(observed, other, 0, keepdims=False)
                innov_rows = lax.dynamic_index_in_dim(innovations, other, 0, keepdims=False)
                partner_xy = lax.dynamic_index_in_dim(obs_xy, other, 1, keepdims=False)
                spread_row = lax.dynamic_index_in_dim(spread, other, 0, keepdims=False)
                gain = pair_gain(x_rows, obs_rows, node_xy, partner_xy, spread_row, float(slot - RADIUS), members)
                return current + jnp.dot(gain, innov_rows, preferred_element_type=jnp.float32)

            def unchanged(current):
                return current
            flag = lax.dynamic_index_in_dim(lax.dynamic_index_in_dim(in_radius, district, 0, keepdims=False), slot, 0, keepdims=False)
            total = lax.cond(flag > 0, accumulate, unchanged, total)
        return total
    return lax.map(one_district, jnp.arange(DISTRICTS, dtype=jnp.int32))
```

```python
import functools
import jax
import jax.numpy as jnp
from jax import lax
from jax.experimental import pallas as pl
from jax.experimental.pallas import tpu as pltpu
from jax.sharding import PartitionSpec as P

BF = jnp.bfloat16
F32 = jnp.float32
VMEM_LIMIT = 62 * 1024 * 1024
PACE = 1.0
WHOLE = pl.BlockSpec(memory_space=pltpu.HBM)
CHUNKS = (3, 3, 2)


def params(**more):
    return pltpu.CompilerParams(vmem_limit_bytes=VMEM_LIMIT, **more)


def cost(length):
    nominal = int(length * PACE * 3.69e6)
    return pl.CostEstimate(flops=0, bytes_accessed=nominal, transcendentals=0)


def pick_kernel(node_ref, table_ref, pos_ref, *refs):
    obs_ref, xy_ref = refs[-2:]
    slots, nodes = node_ref.shape[1], table_ref.shape[1]
    here = lax.broadcasted_iota(jnp.int32, (slots, nodes), 1) == node_ref[0]
    hot = jnp.where(here, 1.0, 0.0).astype(BF)
    obs_ref[0] = jnp.dot(hot, table_ref[0], preferred_element_type=F32).astype(BF)
    xy_ref[0] = lax.dot_general(
        pos_ref[0], hot, (((1,), (1,)), ((), ())), preferred_element_type=F32
    ).astype(BF)


def pick(anomalies, obs_node, pos, after):
    count, nodes, width = anomalies.shape
    slots = obs_node.shape[1]
    return pl.pallas_call(
        pick_kernel,
        grid=(count,),
        in_specs=[
            pl.BlockSpec((1, slots, 1), lambda d: (d, 0, 0)),
            pl.BlockSpec((1, nodes, width), lambda d: (d, 0, 0)),
            pl.BlockSpec((1, 2, nodes), lambda d: (d, 0, 0)),
            *[WHOLE] * len(after),
        ],
        out_specs=[
            pl.BlockSpec((1, slots, width), lambda d: (d, 0, 0)),
            pl.BlockSpec((1, 2, slots), lambda d: (d, 0, 0)),
        ],
        out_shape=[
            jax.ShapeDtypeStruct((count, slots, width), BF),
            jax.ShapeDtypeStruct((count, 2, slots), BF),
        ],
        compiler_params=params(),
        cost_estimate=cost(7),
        name="pick",
    )(obs_node[:, :, None], anomalies, pos, *after)


def taper_kernel(reach, first, *refs):
    flags_ref, node_ref, meta_ref = refs[:3]
    out_ref, buf, sem = refs[-3:]
    step, steps = pl.program_id(0), pl.num_programs(0)
    rows, slots = buf.shape[2:]
    tile = min(rows, 64)
    scale = 2.0 / (reach + 2)

    def band(index):
        low, high = jnp.int32(reach), jnp.int32(reach)
        for s in range(reach):
            low = low - flags_ref[first + index, s]
            high = high + flags_ref[first + index, s + reach + 1]
        return low, high + 1

    def copy(index, s):
        half = lax.rem(index, 2)
        return pltpu.make_async_copy(buf.at[half, s], out_ref.at[index, s], sem.at[half, s])

    def drain(index):
        low, high = band(index)
        lax.fori_loop(low, high, lambda s, carry: (copy(index, s).wait(), carry)[1], 0)

    @pl.when(step >= 2)
    def _():
        drain(step - 2)

    low, high = band(step)

    def part(t, carry):
        at = pl.ds(pl.multiple_of(t * tile, tile), tile)
        node = node_ref[0, at, :] * scale
        node_x = jnp.broadcast_to(node[:, 0:1], (tile, slots))
        node_y = jnp.broadcast_to(node[:, 1:2], (tile, slots))

        def pair(s, inner_carry):
            meta = meta_ref[first + step + s].astype(F32)
            delta_x = ((s - reach).astype(F32) + meta[0:1, :]) * scale - node_x
            delta_y = meta[1:2, :] * scale - node_y
            square = delta_x * delta_x + delta_y * delta_y
            inverse = lax.rsqrt(jnp.maximum(square, 1e-30))
            z = square * inverse
            inner = 1.0 + square * (-5.0 / 3.0 + z * (0.625 + z * (0.5 - 0.25 * z)))
            past = jnp.maximum(z - 1.0, 0.0)
            past_square = past * past
            more = past_square * past_square * past * (1.0 / 3.0 + (2.0 / 3.0) * inverse)
            buf[lax.rem(step, 2), s, at, :] = jnp.where(z < 2.0, inner + more, 0.0)
            return inner_carry

        lax.fori_loop(low, high, pair, 0)
        return carry

    lax.fori_loop(0, rows // tile, part, 0)
    lax.fori_loop(low, high, lambda s, carry: (copy(step, s).start(), carry)[1], 0)

    @pl.when(step == steps - 1)
    def _():
        @pl.when(steps >= 2)
        def _():
            drain(step - 1)

        drain(step)


def tapers(first, here, flags, node_xy, meta, reach, after):
    _, rows, _ = node_xy.shape
    slots = meta.shape[2]
    width = flags.shape[1]
    return pl.pallas_call(
        functools.partial(taper_kernel, reach, first),
        grid=(here,),
        in_specs=[
            pl.BlockSpec(memory_space=pltpu.SMEM),
            pl.BlockSpec((1, rows, 2), lambda d: (first + d, 0, 0)),
            pl.BlockSpec(memory_space=pltpu.VMEM),
            *[WHOLE] * len(after),
        ],
        out_specs=WHOLE,
        out_shape=jax.ShapeDtypeStruct((here, width, rows, slots), F32),
        scratch_shapes=[
            pltpu.VMEM((2, width, rows, slots), F32),
            pltpu.SemaphoreType.DMA((2, width)),
        ],
        compiler_params=params(),
        cost_estimate=cost(3 * here),
        name="taper",
    )(flags, node_xy, meta, *after)


def spread_kernel(degrees, obs_ref, meta_ref, out_ref):
    obs = obs_ref[0].astype(F32)
    square = obs * obs
    high = square.astype(BF)
    low = (square - high.astype(F32)).astype(BF)
    ones = jnp.ones((8, obs.shape[1]), BF)
    dims = (((1,), (1,)), ((), ()))
    total = lax.dot_general(ones, high, dims, preferred_element_type=F32)
    total = total + lax.dot_general(ones, low, dims, preferred_element_type=F32)
    var = meta_ref[0, 2:3, :].astype(F32)
    out_ref[0] = meta_ref[0, 3:4, :].astype(F32) / (total[0:1, :] + degrees * var)


def spreads(obs, meta):
    count, slots, members = obs.shape
    return pl.pallas_call(
        functools.partial(spread_kernel, float(members - 1)),
        grid=(count,),
        in_specs=[
            pl.BlockSpec((1, slots, members), lambda e: (e, 0, 0)),
            pl.BlockSpec((1, 4, slots), lambda e: (e, 0, 0)),
        ],
        out_specs=pl.BlockSpec((1, 1, slots), lambda e: (e, 0, 0)),
        out_shape=jax.ShapeDtypeStruct((count, 1, slots), F32),
        compiler_params=params(),
        cost_estimate=cost(0.5 * count),
        name="spread",
    )(obs, meta)


def pair_kernel(first, reach, parts, *refs):
    flags_ref, taper_ref, scale_ref, table_ref = refs[:4]
    obs_refs, innov_refs = refs[4:7], refs[7:10]
    piece_refs = refs[10 : 9 + parts]
    out_ref, x_buf, t_buf, obs_buf, innov_buf, x_sem, sem = refs[-7:]
    step, steps = pl.program_id(0), pl.num_programs(0)
    rows, width = table_ref.shape[1] // parts, table_ref.shape[2]
    slot_count = flags_ref.shape[1]
    own = obs_refs[1].shape[0]
    me = lax.axis_index("mem")

    def x_copy(index, k):
        half = lax.rem(index, 2)
        source = lax.rem(me + parts - k, parts)
        if k == 0:
            block = table_ref.at[first + index, pl.ds(pl.multiple_of(me * rows, rows), rows), :]
        else:
            block = piece_refs[k - 1].at[index]
        return pltpu.make_async_copy(
            block,
            x_buf.at[half, :, pl.ds(pl.multiple_of(source * width, width), width)],
            x_sem.at[half, k],
        )

    def t_copy(index, s):
        half = lax.rem(index, 2)
        return pltpu.make_async_copy(
            taper_ref.at[index, s], t_buf.at[half, s], sem.at[half, s, 0]
        )

    def row_copies(index, s, part, at):
        half = lax.rem(index, 2)
        return (
            pltpu.make_async_copy(
                obs_refs[part].at[at], obs_buf.at[half, s], sem.at[half, s, 1]
            ),
            pltpu.make_async_copy(
                innov_refs[part].at[at], innov_buf.at[half, s], sem.at[half, s, 2]
            ),
        )

    def fetch(index):
        for j in range(parts):
            x_copy(index, j).start()

        def one(s, carry):
            @pl.when(flags_ref[first + index, s] > 0)
            def _():
                t_copy(index, s).start()
                at = first + index + s - reach

                @pl.when(at < 0)
                def _():
                    for copy in row_copies(index, s, 0, at + reach):
                        copy.start()

                @pl.when(jnp.logical_and(at >= 0, at < own))
                def _():
                    for copy in row_copies(index, s, 1, at):
                        copy.start()

                @pl.when(at >= own)
                def _():
                    for copy in row_copies(index, s, 2, at - own):
                        copy.start()

            return carry

        lax.fori_loop(0, slot_count, one, 0)

    @pl.when(step == 0)
    def _():
        fetch(step)

    @pl.when(step + 1 < steps)
    def _():
        fetch(step + 1)

    out_ref[0] = jnp.zeros_like(out_ref[0])
    for j in range(parts):
        x_copy(step, j).wait()
    half = lax.rem(step, 2)

    def compute(s, carry):
        @pl.when(flags_ref[first + step, s] > 0)
        def _():
            t_copy(step, s).wait()
            for copy in row_copies(step, s, 1, 0):
                copy.wait()
            cov = lax.dot_general(
                x_buf[half], obs_buf[half, s], (((1,), (1,)), ((), ())), preferred_element_type=F32
            )
            gain = (t_buf[half, s] * (cov * scale_ref[first + step + s])).astype(BF)
            out_ref[0] += jnp.dot(gain, innov_buf[half, s], preferred_element_type=F32)

        return carry

    lax.fori_loop(0, slot_count, compute, 0)


def pairs(first, flags, taper, scale, table, pieces, obs, innov, out):
    count, nodes, _ = table.shape
    parts = len(pieces) + 1
    here, rows = taper.shape[0], nodes // parts
    slots, members = obs[1].shape[1:]
    slot_count = flags.shape[1]
    reach = (slot_count - 1) // 2
    operands = [flags, taper, scale, table, *obs, *innov, *pieces]
    in_specs = [
        pl.BlockSpec(memory_space=pltpu.SMEM),
        WHOLE,
        pl.BlockSpec(memory_space=pltpu.VMEM),
        *[WHOLE] * (6 + parts),
    ]
    aliases = {}
    if out is not None:
        aliases = {len(operands): 0}
        operands.append(out)
        in_specs.append(WHOLE)
    return pl.pallas_call(
        functools.partial(pair_kernel, first, reach, parts),
        grid=(here,),
        in_specs=in_specs,
        out_specs=pl.BlockSpec((1, rows, members), lambda i: (first + i, 0, 0)),
        out_shape=jax.ShapeDtypeStruct((count, rows, members), F32),
        scratch_shapes=[
            pltpu.VMEM((2, rows, members), BF),
            pltpu.VMEM((2, slot_count, rows, slots), F32),
            pltpu.VMEM((2, slot_count, slots, members), BF),
            pltpu.VMEM((2, slot_count, slots, members), BF),
            pltpu.SemaphoreType.DMA((2, parts)),
            pltpu.SemaphoreType.DMA((2, slot_count, 3)),
        ],
        input_output_aliases=aliases,
        compiler_params=params(),
        cost_estimate=cost(3 * here),
        name="pairs",
    )(*operands)


def move(copies):
    for load, _ in copies:
        load.start()
    for load, store in copies:
        load.wait()
        store.start()
    for _, store in copies:
        store.wait()


def mover(kernel, shape, buffer, operands, name):
    return pl.pallas_call(
        kernel,
        in_specs=[WHOLE] * len(operands),
        out_specs=WHOLE,
        out_shape=jax.ShapeDtypeStruct(shape, BF),
        scratch_shapes=[
            pltpu.VMEM(buffer, BF),
            pltpu.SemaphoreType.DMA((2, *buffer[:-2])),
        ],
        compiler_params=params(),
        cost_estimate=cost(2),
        name=name,
    )(*operands)


def relay_kernel(*refs):
    p1, p2, p3 = refs[:3]
    out_ref, buf, sem = refs[-3:]
    me = lax.axis_index("mem")
    count = p1.shape[0]

    def run(p4):
        move([
            (
                pltpu.make_async_copy(src.at[i], buf.at[k, i], sem.at[0, k, i]),
                pltpu.make_async_copy(buf.at[k, i], out_ref.at[k, i], sem.at[1, k, i]),
            )
            for k, src in enumerate((p4, p3))
            for i in range(count)
        ])

    @pl.when(me == 2)
    def _():
        run(p1)

    @pl.when(me != 2)
    def _():
        run(p2)


def relay(p1, p2, p3, after):
    shape = (2, *p1.shape)
    return mover(relay_kernel, shape, shape, (p1, p2, p3, *after), "relay")


def place_kernel(*refs):
    own, p1, p2, p3, far = refs[:5]
    out_ref, buf, sem = refs[-3:]
    me = lax.axis_index("mem")
    count, _, width = own.shape
    p4, p5 = far.at[0], far.at[1]
    table = (
        (own, p2, p4, p5),
        (p1, own, p2, p3),
        (p3, p1, own, p2),
        (p5, p4, p1, own),
    )
    for z, sources in enumerate(table):

        @pl.when(me == z)
        def _(sources=sources):
            move([
                (
                    pltpu.make_async_copy(src.at[i], buf.at[j, i], sem.at[0, j, i]),
                    pltpu.make_async_copy(
                        buf.at[j, i],
                        out_ref.at[i, :, j * width : (j + 1) * width],
                        sem.at[1, j, i],
                    ),
                )
                for i in range(count)
                for j, src in enumerate(sources)
            ])


def place(own, near, far, after):
    count, slots, width = own.shape
    return mover(
        place_kernel,
        (count, slots, 4 * width),
        (4, count, slots, width),
        (own, *near, far, *after),
        "place",
    )


def first_hops(block):
    p1 = lax.ppermute(block, "mem", [(0, 1), (1, 2), (2, 3)])
    p2 = lax.ppermute(block, "mem", [(1, 0), (2, 1), (3, 2)])
    p3 = lax.ppermute(block, "mem", [(0, 2), (3, 1)])
    return p1, p2, p3


def last_hop(block):
    return lax.ppermute(block, "mem", [(2, 3), (1, 0)])


def halo(array, reach):
    devices = lax.axis_size("dist")
    up = [(i, i + 1) for i in range(devices - 1)]
    down = [(i + 1, i) for i in range(devices - 1)]
    before = lax.ppermute(array[-reach:], "dist", up)
    after = lax.ppermute(array[:reach], "dist", down)
    return before, array, after


def on_device(anomalies, innovations, obs_var, node_pos, obs_node, obs_count, in_radius):
    count, nodes, width = anomalies.shape
    slots = obs_node.shape[1]
    reach = (in_radius.shape[1] - 1) // 2
    parts = lax.axis_size("mem")
    me = lax.axis_index("mem")
    rows = nodes // parts
    chunks = CHUNKS if sum(CHUNKS) == count else (1,) * count
    starts = [sum(chunks[:c]) for c in range(len(chunks))]
    last = len(chunks) - 1
    sent, taper = {}, {}

    def send(c, k):
        target = lax.rem(me + k, parts)
        block = lax.dynamic_slice(
            anomalies, (starts[c], target * rows, 0), (chunks[c], rows, width)
        )
        shift = [(i, (i + k) % parts) for i in range(parts)]
        sent[c, k] = lax.ppermute(block, "mem", shift)
        return sent[c, k]

    def weigh(c, *after):
        taper[c] = tapers(starts[c], chunks[c], in_radius, node_xy, ext_meta, reach, after)
        return taper[c]

    pos = jnp.transpose(node_pos, (1, 0, 2))
    observed, obs_xy = pick(anomalies, obs_node, pos, ())
    live = jnp.arange(slots, dtype=jnp.int32)[None, :] < obs_count[:, None]
    meta = jnp.concatenate([obs_xy, obs_var[:, None, :], live[:, None, :].astype(BF)], axis=1)
    ext_meta = jnp.concatenate(halo(meta, reach), axis=0)
    node_xy = lax.dynamic_slice_in_dim(node_pos, me * rows, rows, 2)
    node_xy = jnp.transpose(node_xy, (1, 2, 0)).astype(F32)

    if parts == 4:
        near_innov = first_hops(innovations)
        near_obs = first_hops(observed)
        last_taper = weigh(0)
        relay_innov = relay(*near_innov, (last_taper,))
        far_innov = last_hop(relay_innov)
        last_taper = weigh(1, relay_innov, send(0, 2))
        relay_obs = relay(*near_obs, (last_taper,))
        far_obs = last_hop(relay_obs)
        last_taper = weigh(2, relay_obs)
        full_innov = place(innovations, near_innov, far_innov, (last_taper,))
        full_obs = place(
            observed, near_obs, far_obs, (full_innov, send(0, 1), send(0, 3))
        )
        all_innov = halo(full_innov, reach)
        all_obs = halo(full_obs, reach)
    else:
        full_innov = lax.all_gather(innovations, "mem", axis=2, tiled=True)
        full_obs = lax.all_gather(observed, "mem", axis=2, tiled=True)
        all_innov = halo(full_innov, reach)
        all_obs = halo(full_obs, reach)
        for c in range(len(chunks)):
            weigh(c)
    for c in range(len(chunks)):
        for k in range(1, parts):
            if (c, k) not in sent:
                send(c, k)
    low, high = count + reach, count + 2 * reach
    metas = (ext_meta[:reach], ext_meta[reach:low], ext_meta[low:high])
    scale = jnp.concatenate([spreads(o, m) for o, m in zip(all_obs, metas)], axis=0)

    out = None
    for c in range(len(chunks)):
        pieces = [sent[c, k] for k in range(1, parts)]
        out = pairs(
            starts[c], in_radius, taper[c], scale, anomalies, pieces, all_obs, all_innov, out
        )
    return out


def solution(mesh):
    return jax.shard_map(
        on_device,
        mesh=mesh,
        in_specs=(
            P("dist", None, "mem"),
            P("dist", None, "mem"),
            P("dist", None),
            P(None, "dist", None),
            P("dist", None),
            P("dist"),
            P("dist", None),
        ),
        out_specs=P("dist", "mem", None),
        check_vma=False,
    )
```

```python
import functools
import jax
import jax.numpy as jnp
from jax import lax
from jax.experimental import pallas as pl
from jax.experimental.pallas import tpu as pltpu
from jax.sharding import PartitionSpec as P

BF = jnp.bfloat16
F32 = jnp.float32
VMEM_LIMIT = 62 * 1024 * 1024
SPREAD_COST = 30
PACE = 1.0
WHOLE = pl.BlockSpec(memory_space=pltpu.HBM)
CHUNKS = (5, 3)


def params(**more):
    return pltpu.CompilerParams(vmem_limit_bytes=VMEM_LIMIT, **more)


def cost(length):
    nominal = int(length * PACE * 3.69e6)
    return pl.CostEstimate(flops=nominal * 312, bytes_accessed=nominal, transcendentals=0)


def pick_kernel(node_ref, table_ref, pos_ref, *refs):
    obs_ref, xy_ref = refs[-2:]
    slots, nodes = node_ref.shape[1], table_ref.shape[1]
    here = lax.broadcasted_iota(jnp.int32, (slots, nodes), 1) == node_ref[0]
    hot = jnp.where(here, 1.0, 0.0).astype(BF)
    obs_ref[0] = jnp.dot(hot, table_ref[0], preferred_element_type=F32).astype(BF)
    xy_ref[0] = lax.dot_general(
        pos_ref[0], hot, (((1,), (1,)), ((), ())), preferred_element_type=F32
    ).astype(BF)


def pick(anomalies, obs_node, pos, after):
    count, nodes, width = anomalies.shape
    slots = obs_node.shape[1]
    return pl.pallas_call(
        pick_kernel,
        grid=(count,),
        in_specs=[
            pl.BlockSpec((1, slots, 1), lambda d: (d, 0, 0)),
            pl.BlockSpec((1, nodes, width), lambda d: (d, 0, 0)),
            pl.BlockSpec((1, 2, nodes), lambda d: (d, 0, 0)),
            *[WHOLE] * len(after),
        ],
        out_specs=[
            pl.BlockSpec((1, slots, width), lambda d: (d, 0, 0)),
            pl.BlockSpec((1, 2, slots), lambda d: (d, 0, 0)),
        ],
        out_shape=[
            jax.ShapeDtypeStruct((count, slots, width), BF),
            jax.ShapeDtypeStruct((count, 2, slots), BF),
        ],
        compiler_params=params(),
        cost_estimate=cost(7),
        name="pick",
    )(obs_node[:, :, None], anomalies, pos, *after)


def taper_kernel(reach, first, *refs):
    flags_ref, node_ref, meta_ref = refs[:3]
    out_ref, buf, sem = refs[-3:]
    step, steps = pl.program_id(0), pl.num_programs(0)
    rows, slots = buf.shape[2:]
    tile = min(rows, 64)
    scale = 2.0 / (reach + 2)

    def band(index):
        low, high = jnp.int32(reach), jnp.int32(reach)
        for s in range(reach):
            low = low - flags_ref[first + index, s]
            high = high + flags_ref[first + index, s + reach + 1]
        return low, high + 1

    def copy(index, s):
        half = lax.rem(index, 2)
        return pltpu.make_async_copy(buf.at[half, s], out_ref.at[index, s], sem.at[half, s])

    def drain(index):
        low, high = band(index)
        lax.fori_loop(low, high, lambda s, carry: (copy(index, s).wait(), carry)[1], 0)

    @pl.when(step >= 2)
    def _():
        drain(step - 2)

    low, high = band(step)

    def part(t, carry):
        at = pl.ds(pl.multiple_of(t * tile, tile), tile)
        node = node_ref[0, at, :] * scale
        node_x = jnp.broadcast_to(node[:, 0:1], (tile, slots))
        node_y = jnp.broadcast_to(node[:, 1:2], (tile, slots))

        def pair(s, inner_carry):
            meta = meta_ref[first + step + s].astype(F32)
            delta_x = ((s - reach).astype(F32) + meta[0:1, :]) * scale - node_x
            delta_y = meta[1:2, :] * scale - node_y
            square = delta_x * delta_x + delta_y * delta_y
            inverse = lax.rsqrt(jnp.maximum(square, 1e-30))
            z = square * inverse
            inner = 1.0 + square * (-5.0 / 3.0 + z * (0.625 + z * (0.5 - 0.25 * z)))
            past = jnp.maximum(z - 1.0, 0.0)
            past_square = past * past
            more = past_square * past_square * past * (1.0 / 3.0 + (2.0 / 3.0) * inverse)
            buf[lax.rem(step, 2), s, at, :] = jnp.where(z < 2.0, inner + more, 0.0)
            return inner_carry

        lax.fori_loop(low, high, pair, 0)
        return carry

    lax.fori_loop(0, rows // tile, part, 0)
    lax.fori_loop(low, high, lambda s, carry: (copy(step, s).start(), carry)[1], 0)

    @pl.when(step == steps - 1)
    def _():
        @pl.when(steps >= 2)
        def _():
            drain(step - 1)

        drain(step)


def tapers(first, here, flags, node_xy, meta, reach, after):
    _, rows, _ = node_xy.shape
    slots = meta.shape[2]
    width = flags.shape[1]
    return pl.pallas_call(
        functools.partial(taper_kernel, reach, first),
        grid=(here,),
        in_specs=[
            pl.BlockSpec(memory_space=pltpu.SMEM),
            pl.BlockSpec((1, rows, 2), lambda d: (first + d, 0, 0)),
            pl.BlockSpec(memory_space=pltpu.VMEM),
            *[WHOLE] * len(after),
        ],
        out_specs=WHOLE,
        out_shape=jax.ShapeDtypeStruct((here, width, rows, slots), F32),
        scratch_shapes=[
            pltpu.VMEM((2, width, rows, slots), F32),
            pltpu.SemaphoreType.DMA((2, width)),
        ],
        compiler_params=params(),
        cost_estimate=cost(3 * here),
        name="taper",
    )(flags, node_xy, meta, *after)


def spread_row(obs, meta, degrees):
    slots, members = obs.shape
    lanes = min(members, 128)
    total = jnp.zeros((slots, lanes), F32)
    for j in range(members // lanes):
        block = obs[:, j * lanes : (j + 1) * lanes].astype(F32)
        total = total + block * block
    ones = jnp.ones((8, lanes), BF)
    row = jnp.zeros((8, slots), F32)
    for _ in range(3):
        part = total.astype(BF)
        total = total - part.astype(F32)
        row = row + lax.dot_general(
            ones, part, (((1,), (1,)), ((), ())), preferred_element_type=F32
        )
    return meta[3:4, :].astype(F32) / (row[0:1, :] + degrees * meta[2:3, :].astype(F32))


def own_spread_kernel(reach, degrees, obs_ref, meta_ref, *refs):
    out_ref = refs[-1]
    for d in range(obs_ref.shape[0]):
        out_ref[d] = spread_row(obs_ref[d], meta_ref[reach + d], degrees)


def own_spread(obs, meta, reach, after):
    count, slots, members = obs.shape
    vmem = pl.BlockSpec(memory_space=pltpu.VMEM)
    return pl.pallas_call(
        functools.partial(own_spread_kernel, reach, float(members - 1)),
        in_specs=[vmem, vmem, *[WHOLE] * len(after)],
        out_specs=vmem,
        out_shape=jax.ShapeDtypeStruct((count, 1, slots), F32),
        compiler_params=params(),
        cost_estimate=cost(SPREAD_COST),
        name="own_spread",
    )(obs, meta, *after)


def all_spread_kernel(degrees, before_ref, after_ref, own_ref, meta_ref, out_ref):
    reach, count = before_ref.shape[1], own_ref.shape[0]
    out_ref[reach : reach + count] = own_ref[...]
    for d in range(reach):
        out_ref[d] = spread_row(before_ref[0, d], meta_ref[d], degrees)
        e = reach + count + d
        out_ref[e] = spread_row(after_ref[0, d], meta_ref[e], degrees)


def all_spread(edges, own, meta):
    _, reach, slots, members = edges[0].shape
    edge = pl.BlockSpec((1, reach, slots, members), lambda i: (1, 0, 0, 0))
    return pl.pallas_call(
        functools.partial(all_spread_kernel, float(members - 1)),
        grid=(1,),
        in_specs=[
            edge,
            edge,
            pl.BlockSpec(own.shape, lambda i: (0, 0, 0)),
            pl.BlockSpec(meta.shape, lambda i: (0, 0, 0)),
        ],
        out_specs=pl.BlockSpec((meta.shape[0], 1, slots), lambda i: (0, 0, 0)),
        out_shape=jax.ShapeDtypeStruct((meta.shape[0], 1, slots), F32),
        compiler_params=params(),
        cost_estimate=cost(4),
        name="all_spread",
    )(*edges, own, meta)


def pair_kernel(first, reach, here, parts, routes, bases, *refs):
    flags_ref, taper_ref, scale_ref, table_ref = refs[:4]
    before_ref, after_ref, obs_ref, innov_ref = refs[4:8]
    obs_refs = (before_ref.at[1], obs_ref, after_ref.at[1])
    innov_refs = (before_ref.at[0], innov_ref, after_ref.at[0])
    piece_refs = refs[8 : 8 + len(bases)]
    out_ref, x_buf, t_buf, obs_buf, innov_buf, total, x_sem, sem, out_sem = refs[-9:]
    rows, width = table_ref.shape[1] // parts, table_ref.shape[2]
    own, slots = obs_ref.shape[:2]
    me = lax.axis_index("mem")

    def band(index):
        low, high = jnp.int32(reach), jnp.int32(reach)
        for s in range(reach):
            low = low - flags_ref[first + index, s]
            high = high + flags_ref[first + index, s + reach + 1]
        return low, high + 1

    def x_copy(index, j, block):
        half = lax.rem(index, 2)
        return pltpu.make_async_copy(
            block, x_buf.at[half, :, j * width : (j + 1) * width], x_sem.at[half, j]
        )

    def x_start(index, j):
        @pl.when(me == j)
        def _():
            x_copy(index, j, table_ref.at[first + index, j * rows : (j + 1) * rows, :]).start()

        for r, base in enumerate(bases):
            takers = [z for z in range(parts) if routes.get((z, j)) == r]
            if takers:
                wanted = functools.reduce(jnp.logical_or, [me == z for z in takers])

                @pl.when(wanted)
                def _(r=r, base=base):
                    if len(piece_refs[r].shape) == 4:
                        block = piece_refs[r].at[j, first - base + index]
                    else:
                        at = pl.multiple_of((first - base + index) * rows, rows)
                        block = piece_refs[r].at[pl.ds(at, rows)]
                    x_copy(index, j, block).start()

    def t_copy(index, s):
        half = lax.rem(index, 2)
        return pltpu.make_async_copy(
            taper_ref.at[index, s], t_buf.at[half, s], sem.at[half, s, 0]
        )

    def row_copies(index, s, part, at):
        half = lax.rem(index, 2)
        here_rows = pl.ds(pl.multiple_of(s * slots, slots), slots)
        return (
            pltpu.make_async_copy(
                obs_refs[part].at[at], obs_buf.at[half, here_rows], sem.at[half, s, 1]
            ),
            pltpu.make_async_copy(
                innov_refs[part].at[at], innov_buf.at[half, here_rows], sem.at[half, s, 2]
            ),
        )

    def out_copy(index):
        half = lax.rem(index, 2)
        return pltpu.make_async_copy(total.at[half], out_ref.at[first + index], out_sem.at[half])

    def fetch(index):
        for j in range(parts):
            x_start(index, j)
        low, high = band(index)

        def one(s, carry):
            t_copy(index, s).start()
            at = first + index + s - reach

            @pl.when(at < 0)
            def _():
                for copy in row_copies(index, s, 0, at + reach):
                    copy.start()

            @pl.when(jnp.logical_and(at >= 0, at < own))
            def _():
                for copy in row_copies(index, s, 1, at):
                    copy.start()

            @pl.when(at >= own)
            def _():
                for copy in row_copies(index, s, 2, at - own):
                    copy.start()

            return carry

        lax.fori_loop(low, high, one, 0)

    def district(index, carry):
        half = lax.rem(index, 2)

        @pl.when(index + 1 < here)
        def _():
            fetch(index + 1)

        @pl.when(index >= 2)
        def _():
            out_copy(index - 2).wait()

        for j in range(parts):
            x_copy(index, j, table_ref.at[0, 0:rows, :]).wait()
        low, high = band(index)
        odd = lax.rem(high - low, 2)

        def step(s, taken):
            for j in range(taken):
                t_copy(index, s + j).wait()
                for copy in row_copies(index, s + j, 1, 0):
                    copy.wait()
            at = pl.ds(pl.multiple_of(s * slots, slots), taken * slots)
            cov = lax.dot_general(
                x_buf[half], obs_buf[half, at], (((1,), (1,)), ((), ())), preferred_element_type=F32
            )
            gains = [
                (
                    t_buf[half, s + j]
                    * (cov[:, j * slots : (j + 1) * slots] * scale_ref[first + index + s + j])
                ).astype(BF)
                for j in range(taken)
            ]
            gain = gains[0] if taken == 1 else jnp.concatenate(gains, axis=1)
            return jnp.dot(gain, innov_buf[half, at], preferred_element_type=F32)

        @pl.when(odd == 1)
        def _():
            total[half] = step(low, 1)

        @pl.when(odd == 0)
        def _():
            total[half] = step(low, 2)

        def two(i, inner_carry):
            total[half] += step(low + 2 - odd + 2 * i, 2)
            return inner_carry

        lax.fori_loop(0, (high - low - 2 + odd) // 2, two, 0)
        out_copy(index).start()
        return carry

    fetch(0)
    lax.fori_loop(0, here, district, 0)
    for index in range(max(here - 2, 0), here):
        out_copy(index).wait()


def pairs(first, flags, taper, scale, table, pieces, routes, edges, obs, innov, out):
    count = table.shape[0]
    here, _, rows, _ = taper.shape
    parts = table.shape[1] // rows
    bases = [base for _, base in pieces]
    slots, members = obs.shape[1:]
    slot_count = flags.shape[1]
    reach = (slot_count - 1) // 2
    operands = [flags, taper, scale, table, *edges, obs, innov, *[array for array, _ in pieces]]
    in_specs = [
        pl.BlockSpec(memory_space=pltpu.SMEM),
        WHOLE,
        pl.BlockSpec(memory_space=pltpu.VMEM),
        *[WHOLE] * (5 + len(pieces)),
    ]
    aliases = {}
    if out is not None:
        aliases = {len(operands): 0}
        operands.append(out)
        in_specs.append(WHOLE)
    return pl.pallas_call(
        functools.partial(pair_kernel, first, reach, here, parts, routes, bases),
        in_specs=in_specs,
        out_specs=WHOLE,
        out_shape=jax.ShapeDtypeStruct((count, rows, members), F32),
        scratch_shapes=[
            pltpu.VMEM((2, rows, members), BF),
            pltpu.VMEM((2, slot_count, rows, slots), F32),
            pltpu.VMEM((2, slot_count * slots, members), BF),
            pltpu.VMEM((2, slot_count * slots, members), BF),
            pltpu.VMEM((2, rows, members), F32),
            pltpu.SemaphoreType.DMA((2, parts)),
            pltpu.SemaphoreType.DMA((2, slot_count, 3)),
            pltpu.SemaphoreType.DMA((2,)),
        ],
        input_output_aliases=aliases,
        compiler_params=params(),
        cost_estimate=cost(3 * here),
        name="pairs",
    )(*operands)


def move(copies):
    for load, _ in copies:
        load.start()
    for load, store in copies:
        load.wait()
        store.start()
    for _, store in copies:
        store.wait()


def mover(kernel, shape, buffer, operands, name):
    return pl.pallas_call(
        kernel,
        in_specs=[WHOLE] * len(operands),
        out_specs=WHOLE,
        out_shape=jax.ShapeDtypeStruct(shape, BF),
        scratch_shapes=[
            pltpu.VMEM(buffer, BF),
            pltpu.SemaphoreType.DMA((2, *buffer[:-2])),
        ],
        compiler_params=params(),
        cost_estimate=cost(2),
        name=name,
    )(*operands)


def cut_kernel(start, targets, extra, *refs):
    table_ref = refs[0]
    out_ref, buf, sem = refs[-3:]
    parts = len(targets)
    rows = table_ref.shape[1] // parts
    size = (out_ref.shape[0] - extra) // rows
    me = lax.axis_index("mem")

    def run(target):
        copies = []
        for i in range(size):
            src = table_ref.at[start + i, target * rows : (target + 1) * rows, :]
            copies.append((src, slice(i * rows, (i + 1) * rows)))
        for i in range(refs[1].shape[0] if extra else 0):
            slots = refs[1].shape[1]
            first = size * rows + i * slots
            copies.append((refs[1].at[i], slice(first, first + slots)))
        move([
            (
                pltpu.make_async_copy(src, buf.at[to], sem.at[0, n]),
                pltpu.make_async_copy(buf.at[to], out_ref.at[to], sem.at[1, n]),
            )
            for n, (src, to) in enumerate(copies)
        ])

    for target in sorted(set(targets)):
        senders = [z for z in range(parts) if targets[z] == target]
        here = functools.reduce(jnp.logical_or, [me == z for z in senders])

        @pl.when(here)
        def _(target=target):
            run(target)


def cut(table, start, size, targets, extra, after, length=2):
    rows, width = table.shape[1] // len(targets), table.shape[2]
    blocks = (table,) if extra is None else (table, extra)
    more = 0 if extra is None else extra.shape[0] * extra.shape[1]
    shape = (size * rows + more, width)
    operands = (*blocks, *after)
    return pl.pallas_call(
        functools.partial(cut_kernel, start, targets, more),
        in_specs=[WHOLE] * len(operands),
        out_specs=WHOLE,
        out_shape=jax.ShapeDtypeStruct(shape, BF),
        scratch_shapes=[
            pltpu.VMEM(shape, BF),
            pltpu.SemaphoreType.DMA((2, size + (0 if extra is None else extra.shape[0]))),
        ],
        compiler_params=params(),
        cost_estimate=cost(length),
        name="cut",
    )(*operands)


def cut_all_kernel(start, *refs):
    table_ref = refs[0]
    out_ref, buf, sem = refs[-3:]
    parts, size = out_ref.shape[0], out_ref.shape[1]
    rows = out_ref.shape[2]
    move([
        (
            pltpu.make_async_copy(
                table_ref.at[start + i, j * rows : (j + 1) * rows, :], buf.at[j, i], sem.at[0, j, i]
            ),
            pltpu.make_async_copy(buf.at[j, i], out_ref.at[j, i], sem.at[1, j, i]),
        )
        for j in range(parts)
        for i in range(size)
    ])


def cut_all(table, start, size, parts, after):
    shape = (parts, size, table.shape[1] // parts, table.shape[2])
    return mover(functools.partial(cut_all_kernel, start), shape, shape, (table, *after), "cut_all")


def slots_of(ref, i, count, slots):
    if len(ref.shape) == 3:
        return ref.at[i]
    first = ref.shape[0] - (count - i) * slots
    return ref.at[first : first + slots]


def relay_kernel(*refs):
    p1, p2, p3 = refs[:3]
    out_ref, buf, sem = refs[-3:]
    me = lax.axis_index("mem")
    count, slots, _ = p3.shape

    def run(p4):
        move([
            (
                pltpu.make_async_copy(
                    slots_of(src, i, count, slots), buf.at[k, i], sem.at[0, k, i]
                ),
                pltpu.make_async_copy(buf.at[k, i], out_ref.at[k, i], sem.at[1, k, i]),
            )
            for k, src in enumerate((p4, p3))
            for i in range(count)
        ])

    @pl.when(me == 2)
    def _():
        run(p1)

    @pl.when(me != 2)
    def _():
        run(p2)


def relay(p1, p2, p3, after):
    shape = (2, *p3.shape)
    return mover(relay_kernel, shape, shape, (p1, p2, p3, *after), "relay")


def place_kernel(edges, *refs):
    own, p1, p2, p3, far = refs[:5]
    me = lax.axis_index("mem")
    count, slots, width = own.shape
    if edges:
        other = refs[5]
        out_ref, last_ref, first_ref, buf, edge, sem, edge_sem = refs[-7:]
        sides = [(first_ref, 0), (last_ref, count - edges)]
        for n, (_, at) in enumerate(sides):
            pltpu.make_async_copy(
                other.at[at : at + edges], edge.at[n], edge_sem.at[0, n]
            ).start()
    else:
        out_ref, buf, sem = refs[-3:]
        sides = []
    p4, p5 = far.at[0], far.at[1]
    table = (
        (own, p2, p4, p5),
        (p1, own, p2, p3),
        (p3, p1, own, p2),
        (p5, p4, p1, own),
    )
    order = list(range(count))
    for z, sources in enumerate(table):

        @pl.when(me == z)
        def _(sources=sources):
            copies = []
            for i in order:
                for j, src in enumerate(sources):
                    copies.append((
                        pltpu.make_async_copy(
                            slots_of(src, i, count, slots), buf.at[j, i], sem.at[0, j, i]
                        ),
                        pltpu.make_async_copy(
                            buf.at[j, i],
                            out_ref.at[i, :, j * width : (j + 1) * width],
                            sem.at[1, j, i],
                        ),
                    ))
            move(copies)

    copies = []
    for n, (side_ref, at) in enumerate(sides):
        pltpu.make_async_copy(other.at[at : at + edges], edge.at[n], edge_sem.at[0, n]).wait()
        copies.append(pltpu.make_async_copy(edge.at[n], side_ref.at[0], edge_sem.at[1, n]))
        for d in range(edges):
            for j in range(4):
                copies.append(
                    pltpu.make_async_copy(
                        buf.at[j, at + d],
                        side_ref.at[1, d, :, j * width : (j + 1) * width],
                        sem.at[n, j, d],
                    )
                )
    for copy in copies:
        copy.start()
    for copy in copies:
        copy.wait()


def place(own, near, far, edges, after):
    count, slots, width = own.shape
    operands = (own, *near, far, *after)
    shapes = [jax.ShapeDtypeStruct((count, slots, 4 * width), BF)]
    scratch = [pltpu.VMEM((4, count, slots, width), BF)]
    sems = [pltpu.SemaphoreType.DMA((2, 4, count))]
    if edges:
        shapes += [jax.ShapeDtypeStruct((2, edges, slots, 4 * width), BF)] * 2
        scratch.append(pltpu.VMEM((2, edges, slots, 4 * width), BF))
        sems.append(pltpu.SemaphoreType.DMA((2, 2)))
    return pl.pallas_call(
        functools.partial(place_kernel, edges),
        in_specs=[WHOLE] * len(operands),
        out_specs=[WHOLE] * len(shapes),
        out_shape=shapes,
        scratch_shapes=scratch + sems,
        compiler_params=params(),
        cost_estimate=cost(0.1 if edges else 3),
        name="place",
    )(*operands)


def pass_kernel(*refs):
    refs[-1][...] = refs[0][...]


def passed(array, after):
    vmem = pl.BlockSpec(memory_space=pltpu.VMEM)
    return pl.pallas_call(
        pass_kernel,
        in_specs=[vmem] + [WHOLE] * len(after),
        out_specs=vmem,
        out_shape=jax.ShapeDtypeStruct(array.shape, array.dtype),
        compiler_params=params(),
        cost_estimate=cost(0.1),
        name="passed",
    )(array, *after)


UP = ((0, 1), (1, 2), (2, 3))
DOWN = ((1, 0), (2, 1), (3, 2))


def hop(block, pairs_of):
    return lax.ppermute(block, "mem", pairs_of)


def last_hop(block):
    return lax.ppermute(block, "mem", [(2, 3), (1, 0)])


def shifts():
    devices = lax.axis_size("dist")
    up = [(i, i + 1) for i in range(devices - 1)]
    return up, [(j, i) for i, j in up]


def halo(last, first):
    up, down = shifts()
    return lax.ppermute(last, "dist", up), lax.ppermute(first, "dist", down)


def on_device(anomalies, innovations, obs_var, node_pos, obs_node, obs_count, in_radius):
    count, nodes, width = anomalies.shape
    slots = obs_node.shape[1]
    reach = (in_radius.shape[1] - 1) // 2
    parts = lax.axis_size("mem")
    me = lax.axis_index("mem")
    rows = nodes // parts
    chunks = CHUNKS if sum(CHUNKS) == count else (1,) * count
    starts = [sum(chunks[:c]) for c in range(len(chunks))]
    last = len(chunks) - 1
    taper = {}

    def weigh(c, *after):
        taper[c] = tapers(starts[c], chunks[c], in_radius, node_xy, ext_meta, reach, after)
        return taper[c]

    pos = jnp.transpose(node_pos, (1, 0, 2))
    observed, obs_xy = pick(anomalies, obs_node, pos, ())
    live = jnp.arange(slots, dtype=jnp.int32)[None, :] < obs_count[:, None]
    meta = jnp.concatenate([obs_xy, obs_var[:, None, :], live[:, None, :].astype(BF)], axis=1)
    node_xy = lax.dynamic_slice_in_dim(node_pos, me * rows, rows, 2)
    node_xy = jnp.transpose(node_xy, (1, 2, 0)).astype(F32)

    if parts == 4:
        far_pairs = ((0, 2), (3, 1))
        above, below, through = (1, 2, 3, 3), (0, 0, 1, 2), (3, 3, 0, 0)
        near_innov = (
            hop(innovations, UP), hop(innovations, DOWN), hop(innovations, far_pairs)
        )
        up = hop(cut(anomalies, 0, count, above, None, ()), UP)
        down = hop(cut(anomalies, 0, count, below, None, ()), DOWN)
        near_obs = (hop(observed, UP), hop(observed, DOWN), hop(observed, far_pairs))
        relay_innov = relay(*near_innov, ())
        far_innov = last_hop(relay_innov)
        meta = passed(meta, (relay_innov,))
        meta_before, meta_after = halo(meta[-reach:], meta[:reach])
        ext_meta = jnp.concatenate([meta_before, meta, meta_after], axis=0)
        weigh(0, relay_innov, up, down)
        relay_obs = relay(*near_obs, (taper[0],))
        far_obs = last_hop(relay_obs)
        middle = hop(cut(anomalies, 0, count, (2, 2, 1, 1), None, (relay_obs,)), far_pairs)
        (full_innov,) = place(innovations, near_innov, far_innov, 0, (relay_obs,))
        weigh(1, full_innov)
        full_obs, last, first = place(
            observed, near_obs, far_obs, reach, (full_innov, taper[1], middle)
        )
        edges = halo(last, first)
        end_block = cut(anomalies, 0, count, through, None, (full_obs,), 0.1)
        ends = hop(end_block, ((0, 3), (3, 0)))
        cross = [
            hop(cut(anomalies, start, here, through, None, (full_obs,), 0.1), ((1, 3), (2, 0)))
            for start, here in zip(starts, chunks)
        ]
        own_scale = own_spread(full_obs, ext_meta, reach, (ends,))
        pieces = [
            [(up, 0), (down, 0), (middle, 0), (ends, 0), (block, start)]
            for block, start in zip(cross, starts)
        ]
        routes = {
            (1, 0): 0, (2, 1): 0, (3, 2): 0,
            (0, 1): 1, (1, 2): 1, (2, 3): 1,
            (2, 0): 2, (1, 3): 2,
            (3, 0): 3, (0, 3): 3,
            (3, 1): 4, (0, 2): 4,
        }
    else:
        meta_before, meta_after = halo(meta[-reach:], meta[:reach])
        ext_meta = jnp.concatenate([meta_before, meta, meta_after], axis=0)
        full_innov = lax.all_gather(innovations, "mem", axis=2, tiled=True)
        full_obs = lax.all_gather(observed, "mem", axis=2, tiled=True)
        both = jnp.stack([full_innov, full_obs])
        edges = halo(both[:, -reach:], both[:, :reach])
        pieces = []
        for c, (first, size) in enumerate(zip(starts, chunks)):
            weigh(c)
            order = ()
            turns = [[(i, (i + k) % parts) for i in range(parts)] for k in range(1, parts)]
            pieces.append([
                (
                    hop(
                        cut(anomalies, first, size, tuple(t for _, t in turn), None, ()), turn
                    ),
                    first,
                )
                for turn in turns
            ])
        routes = {
            (z, j): (z - j) % parts - 1 for z in range(parts) for j in range(parts) if z != j
        }
    if parts != 4:
        own_scale = own_spread(full_obs, ext_meta, reach, ())
    scale = all_spread(edges, own_scale, ext_meta)

    out = None
    for c in range(len(chunks)):
        out = pairs(
            starts[c],
            in_radius,
            taper[c],
            scale,
            anomalies,
            pieces[c],
            routes,
            edges,
            full_obs,
            full_innov,
            out,
        )
    return out


def solution(mesh):
    return jax.shard_map(
        on_device,
        mesh=mesh,
        in_specs=(
            P("dist", None, "mem"),
            P("dist", None, "mem"),
            P("dist", None),
            P(None, "dist", None),
            P("dist", None),
            P("dist"),
            P("dist", None),
        ),
        out_specs=P("dist", "mem", None),
        check_vma=False,
    )
```

```python
import functools
import jax
import jax.numpy as jnp
from jax import lax
from jax.experimental import pallas as pl
from jax.experimental.pallas import tpu as pltpu
from jax.sharding import PartitionSpec as P

BF = jnp.bfloat16
F32 = jnp.float32
VMEM_LIMIT = 62 * 1024 * 1024
SPREAD_COST = 30
PACE = 1.0
WHOLE = pl.BlockSpec(memory_space=pltpu.HBM)
CHUNKS = (4, 4)


def params(**more):
    return pltpu.CompilerParams(vmem_limit_bytes=VMEM_LIMIT, **more)


def cost(length):
    nominal = int(length * PACE * 3.69e6)
    return pl.CostEstimate(flops=nominal * 312, bytes_accessed=nominal, transcendentals=0)


def pick_kernel(node_ref, table_ref, pos_ref, *refs):
    obs_ref, xy_ref = refs[-2:]
    slots, nodes = node_ref.shape[1], table_ref.shape[1]
    here = lax.broadcasted_iota(jnp.int32, (slots, nodes), 1) == node_ref[0]
    hot = jnp.where(here, 1.0, 0.0).astype(BF)
    obs_ref[0] = jnp.dot(hot, table_ref[0], preferred_element_type=F32).astype(BF)
    xy_ref[0] = lax.dot_general(
        pos_ref[0], hot, (((1,), (1,)), ((), ())), preferred_element_type=F32
    ).astype(BF)


def pick(anomalies, obs_node, pos, after):
    count, nodes, width = anomalies.shape
    slots = obs_node.shape[1]
    return pl.pallas_call(
        pick_kernel,
        grid=(count,),
        in_specs=[
            pl.BlockSpec((1, slots, 1), lambda d: (d, 0, 0)),
            pl.BlockSpec((1, nodes, width), lambda d: (d, 0, 0)),
            pl.BlockSpec((1, 2, nodes), lambda d: (d, 0, 0)),
            *[WHOLE] * len(after),
        ],
        out_specs=[
            pl.BlockSpec((1, slots, width), lambda d: (d, 0, 0)),
            pl.BlockSpec((1, 2, slots), lambda d: (d, 0, 0)),
        ],
        out_shape=[
            jax.ShapeDtypeStruct((count, slots, width), BF),
            jax.ShapeDtypeStruct((count, 2, slots), BF),
        ],
        compiler_params=params(),
        cost_estimate=cost(7),
        name="pick",
    )(obs_node[:, :, None], anomalies, pos, *after)


def taper_kernel(reach, first, *refs):
    flags_ref, node_ref, meta_ref = refs[:3]
    out_ref, buf, sem = refs[-3:]
    step, steps = pl.program_id(0), pl.num_programs(0)
    rows, slots = buf.shape[2:]
    tile = min(rows, 64)
    scale = 2.0 / (reach + 2)

    def band(index):
        low, high = jnp.int32(reach), jnp.int32(reach)
        for s in range(reach):
            low = low - flags_ref[first + index, s]
            high = high + flags_ref[first + index, s + reach + 1]
        return low, high + 1

    def copy(index, s):
        half = lax.rem(index, 2)
        return pltpu.make_async_copy(buf.at[half, s], out_ref.at[index, s], sem.at[half, s])

    def drain(index):
        low, high = band(index)
        lax.fori_loop(low, high, lambda s, carry: (copy(index, s).wait(), carry)[1], 0)

    @pl.when(step >= 2)
    def _():
        drain(step - 2)

    low, high = band(step)

    def part(t, carry):
        at = pl.ds(pl.multiple_of(t * tile, tile), tile)
        node = node_ref[0, at, :] * scale
        node_x = jnp.broadcast_to(node[:, 0:1], (tile, slots))
        node_y = jnp.broadcast_to(node[:, 1:2], (tile, slots))

        def pair(s, inner_carry):
            meta = meta_ref[first + step + s].astype(F32)
            delta_x = ((s - reach).astype(F32) + meta[0:1, :]) * scale - node_x
            delta_y = meta[1:2, :] * scale - node_y
            square = delta_x * delta_x + delta_y * delta_y
            inverse = lax.rsqrt(jnp.maximum(square, 1e-30))
            z = square * inverse
            inner = 1.0 + square * (-5.0 / 3.0 + z * (0.625 + z * (0.5 - 0.25 * z)))
            past = jnp.maximum(z - 1.0, 0.0)
            past_square = past * past
            more = past_square * past_square * past * (1.0 / 3.0 + (2.0 / 3.0) * inverse)
            buf[lax.rem(step, 2), s, at, :] = jnp.where(z < 2.0, inner + more, 0.0)
            return inner_carry

        lax.fori_loop(low, high, pair, 0)
        return carry

    lax.fori_loop(0, rows // tile, part, 0)
    lax.fori_loop(low, high, lambda s, carry: (copy(step, s).start(), carry)[1], 0)

    @pl.when(step == steps - 1)
    def _():
        @pl.when(steps >= 2)
        def _():
            drain(step - 1)

        drain(step)


def tapers(first, here, flags, node_xy, meta, reach, after):
    _, rows, _ = node_xy.shape
    slots = meta.shape[2]
    width = flags.shape[1]
    return pl.pallas_call(
        functools.partial(taper_kernel, reach, first),
        grid=(here,),
        in_specs=[
            pl.BlockSpec(memory_space=pltpu.SMEM),
            pl.BlockSpec((1, rows, 2), lambda d: (first + d, 0, 0)),
            pl.BlockSpec(memory_space=pltpu.VMEM),
            *[WHOLE] * len(after),
        ],
        out_specs=WHOLE,
        out_shape=jax.ShapeDtypeStruct((here, width, rows, slots), F32),
        scratch_shapes=[
            pltpu.VMEM((2, width, rows, slots), F32),
            pltpu.SemaphoreType.DMA((2, width)),
        ],
        compiler_params=params(),
        cost_estimate=cost(3 * here),
        name="taper",
    )(flags, node_xy, meta, *after)


def spread_row(obs, meta, degrees):
    slots, members = obs.shape
    lanes = min(members, 128)
    total = jnp.zeros((slots, lanes), F32)
    for j in range(members // lanes):
        block = obs[:, j * lanes : (j + 1) * lanes].astype(F32)
        total = total + block * block
    ones = jnp.ones((8, lanes), BF)
    row = jnp.zeros((8, slots), F32)
    for _ in range(3):
        part = total.astype(BF)
        total = total - part.astype(F32)
        row = row + lax.dot_general(
            ones, part, (((1,), (1,)), ((), ())), preferred_element_type=F32
        )
    return meta[3:4, :].astype(F32) / (row[0:1, :] + degrees * meta[2:3, :].astype(F32))


def own_spread_kernel(reach, degrees, obs_ref, meta_ref, *refs):
    out_ref = refs[-1]
    for d in range(obs_ref.shape[0]):
        out_ref[d] = spread_row(obs_ref[d], meta_ref[reach + d], degrees)


def own_spread(obs, meta, reach, after):
    count, slots, members = obs.shape
    vmem = pl.BlockSpec(memory_space=pltpu.VMEM)
    return pl.pallas_call(
        functools.partial(own_spread_kernel, reach, float(members - 1)),
        in_specs=[vmem, vmem, *[WHOLE] * len(after)],
        out_specs=vmem,
        out_shape=jax.ShapeDtypeStruct((count, 1, slots), F32),
        compiler_params=params(),
        cost_estimate=cost(SPREAD_COST),
        name="own_spread",
    )(obs, meta, *after)


def all_spread_kernel(degrees, before_ref, after_ref, own_ref, meta_ref, out_ref):
    reach, count = before_ref.shape[0], own_ref.shape[0]
    out_ref[reach : reach + count] = own_ref[...]
    for d in range(reach):
        out_ref[d] = spread_row(before_ref[d], meta_ref[d], degrees)
        e = reach + count + d
        out_ref[e] = spread_row(after_ref[d], meta_ref[e], degrees)


def all_spread(before, after, own, meta):
    slots, members = before.shape[1:]
    return pl.pallas_call(
        functools.partial(all_spread_kernel, float(members - 1)),
        out_shape=jax.ShapeDtypeStruct((meta.shape[0], 1, slots), F32),
        compiler_params=params(),
        cost_estimate=cost(4),
        name="all_spread",
    )(before, after, own, meta)


def pair_kernel(first, reach, here, parts, routes, bases, *refs):
    flags_ref, taper_ref, scale_ref, table_ref = refs[:4]
    obs_refs, innov_refs = refs[4:7], refs[7:10]
    piece_refs = refs[10 : 10 + len(bases)]
    out_ref, x_buf, t_buf, obs_buf, innov_buf, total, x_sem, sem, out_sem = refs[-9:]
    rows, width = table_ref.shape[1] // parts, table_ref.shape[2]
    own, slots = obs_refs[1].shape[:2]
    me = lax.axis_index("mem")

    def band(index):
        low, high = jnp.int32(reach), jnp.int32(reach)
        for s in range(reach):
            low = low - flags_ref[first + index, s]
            high = high + flags_ref[first + index, s + reach + 1]
        return low, high + 1

    def x_copy(index, j, block):
        half = lax.rem(index, 2)
        return pltpu.make_async_copy(
            block, x_buf.at[half, :, j * width : (j + 1) * width], x_sem.at[half, j]
        )

    def x_start(index, j):
        @pl.when(me == j)
        def _():
            x_copy(index, j, table_ref.at[first + index, j * rows : (j + 1) * rows, :]).start()

        for r, base in enumerate(bases):
            takers = [z for z in range(parts) if routes.get((z, j)) == r]
            if takers:
                wanted = functools.reduce(jnp.logical_or, [me == z for z in takers])

                @pl.when(wanted)
                def _(r=r, base=base):
                    if len(piece_refs[r].shape) == 4:
                        block = piece_refs[r].at[j, first - base + index]
                    else:
                        at = pl.multiple_of((first - base + index) * rows, rows)
                        block = piece_refs[r].at[pl.ds(at, rows)]
                    x_copy(index, j, block).start()

    def t_copy(index, s):
        half = lax.rem(index, 2)
        return pltpu.make_async_copy(
            taper_ref.at[index, s], t_buf.at[half, s], sem.at[half, s, 0]
        )

    def row_copies(index, s, part, at):
        half = lax.rem(index, 2)
        here_rows = pl.ds(pl.multiple_of(s * slots, slots), slots)
        return (
            pltpu.make_async_copy(
                obs_refs[part].at[at], obs_buf.at[half, here_rows], sem.at[half, s, 1]
            ),
            pltpu.make_async_copy(
                innov_refs[part].at[at], innov_buf.at[half, here_rows], sem.at[half, s, 2]
            ),
        )

    def out_copy(index):
        half = lax.rem(index, 2)
        return pltpu.make_async_copy(total.at[half], out_ref.at[first + index], out_sem.at[half])

    def fetch(index):
        for j in range(parts):
            x_start(index, j)
        low, high = band(index)

        def one(s, carry):
            t_copy(index, s).start()
            at = first + index + s - reach

            @pl.when(at < 0)
            def _():
                for copy in row_copies(index, s, 0, at + reach):
                    copy.start()

            @pl.when(jnp.logical_and(at >= 0, at < own))
            def _():
                for copy in row_copies(index, s, 1, at):
                    copy.start()

            @pl.when(at >= own)
            def _():
                for copy in row_copies(index, s, 2, at - own):
                    copy.start()

            return carry

        lax.fori_loop(low, high, one, 0)

    def district(index, carry):
        half = lax.rem(index, 2)

        @pl.when(index + 1 < here)
        def _():
            fetch(index + 1)

        @pl.when(index >= 2)
        def _():
            out_copy(index - 2).wait()

        for j in range(parts):
            x_copy(index, j, table_ref.at[0, 0:rows, :]).wait()
        low, high = band(index)
        odd = lax.rem(high - low, 2)

        def step(s, taken):
            for j in range(taken):
                t_copy(index, s + j).wait()
                for copy in row_copies(index, s + j, 1, 0):
                    copy.wait()
            at = pl.ds(pl.multiple_of(s * slots, slots), taken * slots)
            cov = lax.dot_general(
                x_buf[half], obs_buf[half, at], (((1,), (1,)), ((), ())), preferred_element_type=F32
            )
            gains = [
                (
                    t_buf[half, s + j]
                    * (cov[:, j * slots : (j + 1) * slots] * scale_ref[first + index + s + j])
                ).astype(BF)
                for j in range(taken)
            ]
            gain = gains[0] if taken == 1 else jnp.concatenate(gains, axis=1)
            return jnp.dot(gain, innov_buf[half, at], preferred_element_type=F32)

        @pl.when(odd == 1)
        def _():
            total[half] = step(low, 1)

        @pl.when(odd == 0)
        def _():
            total[half] = step(low, 2)

        def two(i, inner_carry):
            total[half] += step(low + 2 - odd + 2 * i, 2)
            return inner_carry

        lax.fori_loop(0, (high - low - 2 + odd) // 2, two, 0)
        out_copy(index).start()
        return carry

    fetch(0)
    lax.fori_loop(0, here, district, 0)
    for index in range(max(here - 2, 0), here):
        out_copy(index).wait()


def pairs(first, flags, taper, scale, table, pieces, routes, obs, innov, out):
    count = table.shape[0]
    here, _, rows, _ = taper.shape
    parts = table.shape[1] // rows
    bases = [base for _, base in pieces]
    slots, members = obs[1].shape[1:]
    slot_count = flags.shape[1]
    reach = (slot_count - 1) // 2
    operands = [flags, taper, scale, table, *obs, *innov, *[array for array, _ in pieces]]
    in_specs = [
        pl.BlockSpec(memory_space=pltpu.SMEM),
        WHOLE,
        pl.BlockSpec(memory_space=pltpu.VMEM),
        *[WHOLE] * (7 + len(pieces)),
    ]
    aliases = {}
    if out is not None:
        aliases = {len(operands): 0}
        operands.append(out)
        in_specs.append(WHOLE)
    return pl.pallas_call(
        functools.partial(pair_kernel, first, reach, here, parts, routes, bases),
        in_specs=in_specs,
        out_specs=WHOLE,
        out_shape=jax.ShapeDtypeStruct((count, rows, members), F32),
        scratch_shapes=[
            pltpu.VMEM((2, rows, members), BF),
            pltpu.VMEM((2, slot_count, rows, slots), F32),
            pltpu.VMEM((2, slot_count * slots, members), BF),
            pltpu.VMEM((2, slot_count * slots, members), BF),
            pltpu.VMEM((2, rows, members), F32),
            pltpu.SemaphoreType.DMA((2, parts)),
            pltpu.SemaphoreType.DMA((2, slot_count, 3)),
            pltpu.SemaphoreType.DMA((2,)),
        ],
        input_output_aliases=aliases,
        compiler_params=params(),
        cost_estimate=cost(3 * here),
        name="pairs",
    )(*operands)


def move(copies):
    for load, _ in copies:
        load.start()
    for load, store in copies:
        load.wait()
        store.start()
    for _, store in copies:
        store.wait()


def mover(kernel, shape, buffer, operands, name):
    return pl.pallas_call(
        kernel,
        in_specs=[WHOLE] * len(operands),
        out_specs=WHOLE,
        out_shape=jax.ShapeDtypeStruct(shape, BF),
        scratch_shapes=[
            pltpu.VMEM(buffer, BF),
            pltpu.SemaphoreType.DMA((2, *buffer[:-2])),
        ],
        compiler_params=params(),
        cost_estimate=cost(2),
        name=name,
    )(*operands)


def cut_kernel(start, targets, extra, *refs):
    table_ref = refs[0]
    out_ref, buf, sem = refs[-3:]
    parts = len(targets)
    rows = table_ref.shape[1] // parts
    size = (out_ref.shape[0] - extra) // rows
    me = lax.axis_index("mem")

    def run(target):
        copies = []
        for i in range(size):
            src = table_ref.at[start + i, target * rows : (target + 1) * rows, :]
            copies.append((src, slice(i * rows, (i + 1) * rows)))
        for i in range(refs[1].shape[0] if extra else 0):
            slots = refs[1].shape[1]
            first = size * rows + i * slots
            copies.append((refs[1].at[i], slice(first, first + slots)))
        move([
            (
                pltpu.make_async_copy(src, buf.at[to], sem.at[0, n]),
                pltpu.make_async_copy(buf.at[to], out_ref.at[to], sem.at[1, n]),
            )
            for n, (src, to) in enumerate(copies)
        ])

    for target in sorted(set(targets)):
        senders = [z for z in range(parts) if targets[z] == target]
        here = functools.reduce(jnp.logical_or, [me == z for z in senders])

        @pl.when(here)
        def _(target=target):
            run(target)


def cut(table, start, size, targets, extra, after, length=2):
    rows, width = table.shape[1] // len(targets), table.shape[2]
    blocks = (table,) if extra is None else (table, extra)
    more = 0 if extra is None else extra.shape[0] * extra.shape[1]
    shape = (size * rows + more, width)
    operands = (*blocks, *after)
    return pl.pallas_call(
        functools.partial(cut_kernel, start, targets, more),
        in_specs=[WHOLE] * len(operands),
        out_specs=WHOLE,
        out_shape=jax.ShapeDtypeStruct(shape, BF),
        scratch_shapes=[
            pltpu.VMEM(shape, BF),
            pltpu.SemaphoreType.DMA((2, size + (0 if extra is None else extra.shape[0]))),
        ],
        compiler_params=params(),
        cost_estimate=cost(length),
        name="cut",
    )(*operands)


def cut_all_kernel(start, *refs):
    table_ref = refs[0]
    out_ref, buf, sem = refs[-3:]
    parts, size = out_ref.shape[0], out_ref.shape[1]
    rows = out_ref.shape[2]
    move([
        (
            pltpu.make_async_copy(
                table_ref.at[start + i, j * rows : (j + 1) * rows, :], buf.at[j, i], sem.at[0, j, i]
            ),
            pltpu.make_async_copy(buf.at[j, i], out_ref.at[j, i], sem.at[1, j, i]),
        )
        for j in range(parts)
        for i in range(size)
    ])


def cut_all(table, start, size, parts, after):
    shape = (parts, size, table.shape[1] // parts, table.shape[2])
    return mover(functools.partial(cut_all_kernel, start), shape, shape, (table, *after), "cut_all")


def slots_of(ref, i, count, slots):
    if len(ref.shape) == 3:
        return ref.at[i]
    first = ref.shape[0] - (count - i) * slots
    return ref.at[first : first + slots]


def relay_kernel(*refs):
    p1, p2, p3 = refs[:3]
    out_ref, buf, sem = refs[-3:]
    me = lax.axis_index("mem")
    count, slots, _ = p3.shape

    def run(p4):
        move([
            (
                pltpu.make_async_copy(
                    slots_of(src, i, count, slots), buf.at[k, i], sem.at[0, k, i]
                ),
                pltpu.make_async_copy(buf.at[k, i], out_ref.at[k, i], sem.at[1, k, i]),
            )
            for k, src in enumerate((p4, p3))
            for i in range(count)
        ])

    @pl.when(me == 2)
    def _():
        run(p1)

    @pl.when(me != 2)
    def _():
        run(p2)


def relay(p1, p2, p3, after):
    shape = (2, *p3.shape)
    return mover(relay_kernel, shape, shape, (p1, p2, p3, *after), "relay")


def place_kernel(edges, *refs):
    own, p1, p2, p3, far = refs[:5]
    me = lax.axis_index("mem")
    count, slots, width = own.shape
    out_ref, last_ref, first_ref, buf, sem = refs[-5:]
    sides = [(first_ref, 0), (last_ref, count - edges)]
    p4, p5 = far.at[0], far.at[1]
    table = (
        (own, p2, p4, p5),
        (p1, own, p2, p3),
        (p3, p1, own, p2),
        (p5, p4, p1, own),
    )
    order = list(range(count))
    for z, sources in enumerate(table):

        @pl.when(me == z)
        def _(sources=sources):
            copies = []
            for i in order:
                for j, src in enumerate(sources):
                    copies.append((
                        pltpu.make_async_copy(
                            slots_of(src, i, count, slots), buf.at[j, i], sem.at[0, j, i]
                        ),
                        pltpu.make_async_copy(
                            buf.at[j, i],
                            out_ref.at[i, :, j * width : (j + 1) * width],
                            sem.at[1, j, i],
                        ),
                    ))
            move(copies)

    copies = [
        pltpu.make_async_copy(
            buf.at[j, at + d], side_ref.at[d, :, j * width : (j + 1) * width], sem.at[n, j, d]
        )
        for n, (side_ref, at) in enumerate(sides)
        for d in range(edges)
        for j in range(4)
    ]
    for copy in copies:
        copy.start()
    for copy in copies:
        copy.wait()


def place(own, near, far, edges, after, length):
    count, slots, width = own.shape
    operands = (own, *near, far, *after)
    shapes = [jax.ShapeDtypeStruct((count, slots, 4 * width), BF)]
    shapes += [jax.ShapeDtypeStruct((edges, slots, 4 * width), BF)] * 2
    scratch = [pltpu.VMEM((4, count, slots, width), BF)]
    sems = [pltpu.SemaphoreType.DMA((2, 4, count))]
    return pl.pallas_call(
        functools.partial(place_kernel, edges),
        in_specs=[WHOLE] * len(operands),
        out_specs=[WHOLE] * len(shapes),
        out_shape=shapes,
        scratch_shapes=scratch + sems,
        compiler_params=params(),
        cost_estimate=cost(length),
        name="place",
    )(*operands)


def pass_kernel(*refs):
    refs[-1][...] = refs[0][...]


def passed(array, after):
    vmem = pl.BlockSpec(memory_space=pltpu.VMEM)
    return pl.pallas_call(
        pass_kernel,
        in_specs=[vmem] + [WHOLE] * len(after),
        out_specs=vmem,
        out_shape=jax.ShapeDtypeStruct(array.shape, array.dtype),
        compiler_params=params(),
        cost_estimate=cost(0.1),
        name="passed",
    )(array, *after)


UP = ((0, 1), (1, 2), (2, 3))
DOWN = ((1, 0), (2, 1), (3, 2))


def hop(block, pairs_of):
    return lax.ppermute(block, "mem", pairs_of)


def last_hop(block):
    return lax.ppermute(block, "mem", [(2, 3), (1, 0)])


def shifts():
    devices = lax.axis_size("dist")
    up = [(i, i + 1) for i in range(devices - 1)]
    return up, [(j, i) for i, j in up]


def halo(last, first):
    up, down = shifts()
    return lax.ppermute(last, "dist", up), lax.ppermute(first, "dist", down)


def on_device(anomalies, innovations, obs_var, node_pos, obs_node, obs_count, in_radius):
    count, nodes, width = anomalies.shape
    slots = obs_node.shape[1]
    reach = (in_radius.shape[1] - 1) // 2
    parts = lax.axis_size("mem")
    me = lax.axis_index("mem")
    rows = nodes // parts
    chunks = CHUNKS if sum(CHUNKS) == count else (1,) * count
    starts = [sum(chunks[:c]) for c in range(len(chunks))]
    last = len(chunks) - 1
    taper = {}

    def weigh(c, *after):
        taper[c] = tapers(starts[c], chunks[c], in_radius, node_xy, ext_meta, reach, after)
        return taper[c]

    pos = jnp.transpose(node_pos, (1, 0, 2))
    observed, obs_xy = pick(anomalies, obs_node, pos, ())
    live = jnp.arange(slots, dtype=jnp.int32)[None, :] < obs_count[:, None]
    meta = jnp.concatenate([obs_xy, obs_var[:, None, :], live[:, None, :].astype(BF)], axis=1)
    node_xy = lax.dynamic_slice_in_dim(node_pos, me * rows, rows, 2)
    node_xy = jnp.transpose(node_xy, (1, 2, 0)).astype(F32)

    if parts == 4:
        far_pairs = ((0, 2), (3, 1))
        above, below, through = (1, 2, 3, 3), (0, 0, 1, 2), (3, 3, 0, 0)
        near_innov = (
            hop(innovations, UP), hop(innovations, DOWN), hop(innovations, far_pairs)
        )
        up = hop(cut(anomalies, 0, count, above, None, ()), UP)
        down = hop(cut(anomalies, 0, count, below, None, ()), DOWN)
        near_obs = (hop(observed, UP), hop(observed, DOWN), hop(observed, far_pairs))
        relay_innov = relay(*near_innov, ())
        far_innov = last_hop(relay_innov)
        meta = passed(meta, (relay_innov,))
        meta_before, meta_after = halo(meta[-reach:], meta[:reach])
        ext_meta = jnp.concatenate([meta_before, meta, meta_after], axis=0)
        weigh(0, relay_innov, up, down)
        relay_obs = relay(*near_obs, (taper[0],))
        far_obs = last_hop(relay_obs)
        middle = hop(cut(anomalies, 0, count, (2, 2, 1, 1), None, (relay_obs,)), far_pairs)
        full_innov, last, first = place(innovations, near_innov, far_innov, reach, (relay_obs,), 3)
        low, high = halo(last, first)
        all_innov = (low, full_innov, high)
        weigh(1, full_innov)
        end_block = cut(anomalies, 0, count, through, None, (full_innov,), 0.1)
        full_obs, last, first = place(
            observed, near_obs, far_obs, reach, (taper[1], middle, low, high), 0.1
        )
        low, high = halo(last, first)
        all_obs = (low, full_obs, high)
        ends = hop(end_block, ((0, 3), (3, 0)))
        cross = [
            hop(cut(anomalies, start, here, through, None, (full_obs,), 0.1), ((1, 3), (2, 0)))
            for start, here in zip(starts, chunks)
        ]
        own_scale = own_spread(full_obs, ext_meta, reach, (ends,))
        pieces = [
            [(up, 0), (down, 0), (middle, 0), (ends, 0), (block, start)]
            for block, start in zip(cross, starts)
        ]
        routes = {
            (1, 0): 0, (2, 1): 0, (3, 2): 0,
            (0, 1): 1, (1, 2): 1, (2, 3): 1,
            (2, 0): 2, (1, 3): 2,
            (3, 0): 3, (0, 3): 3,
            (3, 1): 4, (0, 2): 4,
        }
    else:
        meta_before, meta_after = halo(meta[-reach:], meta[:reach])
        ext_meta = jnp.concatenate([meta_before, meta, meta_after], axis=0)
        full_innov = lax.all_gather(innovations, "mem", axis=2, tiled=True)
        full_obs = lax.all_gather(observed, "mem", axis=2, tiled=True)
        all_innov, all_obs = [
            (low, full, high)
            for full in (full_innov, full_obs)
            for low, high in [halo(full[-reach:], full[:reach])]
        ]
        pieces = []
        for c, (first, size) in enumerate(zip(starts, chunks)):
            weigh(c)
            order = ()
            turns = [[(i, (i + k) % parts) for i in range(parts)] for k in range(1, parts)]
            pieces.append([
                (
                    hop(
                        cut(anomalies, first, size, tuple(t for _, t in turn), None, ()), turn
                    ),
                    first,
                )
                for turn in turns
            ])
        routes = {
            (z, j): (z - j) % parts - 1 for z in range(parts) for j in range(parts) if z != j
        }
    if parts != 4:
        own_scale = own_spread(full_obs, ext_meta, reach, ())
    scale = all_spread(all_obs[0], all_obs[2], own_scale, ext_meta)

    out = None
    for c in range(len(chunks)):
        out = pairs(
            starts[c],
            in_radius,
            taper[c],
            scale,
            anomalies,
            pieces[c],
            routes,
            all_obs,
            all_innov,
            out,
        )
    return out


def solution(mesh):
    return jax.shard_map(
        on_device,
        mesh=mesh,
        in_specs=(
            P("dist", None, "mem"),
            P("dist", None, "mem"),
            P("dist", None),
            P(None, "dist", None),
            P("dist", None),
            P("dist"),
            P("dist", None),
        ),
        out_specs=P("dist", "mem", None),
        check_vma=False,
    )
```
